32 devices in a mesh: tile: 8 (over y, x, core), chan: 4 (over z).
Axes of the slice: x: 2, y: 2, z: 4, core: 2. Of those that a mesh axis runs over, the one named last changes fastest.
Arguments:
- latlon: bfloat16 [1, 2048, 8, 512], P(None, 'tile', None, 'chan'), may hold values from -6 to 6
- remap_weights: bfloat16 [8, 1156, 2048], P('tile'), may hold values from -0.1875 to 0.1875
- term_source: int32 [8, 256], replicated, may hold values from 0 to 7, as said below
- term_block: int32 [8, 256], replicated, may hold values from 0 to 255
- term_count: int32 [8], replicated, may hold values from 0 to 256, as said below
- rotation: int32 [8], P('tile'), may hold values from 0 to 3
- depthwise: bfloat16 [3, 3, 512], P(None, None, 'chan'), may hold values from -2 to 2
- pointwise: bfloat16 [512, 512], replicated, may hold values from -0.25 to 0.25
- cotangent: bfloat16 [1, 8192, 512], P(None, 'tile', 'chan'), may hold values from -6 to 6
Outputs:
- coupled: bfloat16 [1, 8192, 512], P(None, 'tile', 'chan')
- grad_latlon: bfloat16 [1, 2048, 8, 512], P(None, 'tile', None, 'chan')
- grad_depthwise: float32 [3, 3, 512], P(None, None, 'chan')
- grad_pointwise: float32 [512, 512], P('chan')
The draws below stay inside these ranges and needn't reach their ends.
Inputs may be any that keep to these rules, and one draw needn't show every extreme that they name: `term_source`: the first term_count[d] entries of row d name the source tile of each term and the rest are 0. Among the used entries of a row no source tile appears more than 48 times, and some row names a tile exactly 48 times. `term_count`: some face tile uses all 256 terms.
All inputs are finite; a program needn't handle non-finite values.
Results may differ from the reference program's by a relative error of at most 0.0059.
Values may be sent and summed in bfloat16 or wider, within the bound.
A program may use at most 64 MiB of HBM per device.

```python
import jax
import jax.numpy as jnp
from jax import lax

CH = 512
TILE_EDGE = 32
SEG = 8
KMAX = 256
SRC_DEV = 256
BATCH = 1
CAP = 48
SOURCE_BLOCKS = 2048
EXT_CELLS = 1156
TERM_PTS = 2048
TILE_CELLS = 1024
TOTAL_CELLS = 8192
CELLS = 8192
N_TILE = 8


def term_tables(key):
    base_key = jax.random.fold_in(key, 4242)
    key_busy, key_forced, key_heavy, key_light = jax.random.split(base_key, 4)
    tile_ids = jnp.arange(N_TILE)
    busy_rows = jax.random.randint(key_busy, (N_TILE,), 0, 4) == 0
    forced = jax.random.randint(key_forced, (), 0, N_TILE)
    heavy_load = jax.random.randint(key_heavy, (N_TILE, N_TILE), CAP // 2, CAP + 1)
    light_load = jax.random.randint(key_light, (N_TILE, N_TILE), 0, CAP // 3 + 1)
    pair_count = jnp.where(busy_rows[:, None], heavy_load, light_load)
    pair_count = jnp.where((tile_ids == forced)[:, None], CAP, pair_count)
    before = jnp.cumsum(pair_count, axis=1) - pair_count
    pair_count = jnp.minimum(pair_count, jnp.maximum(KMAX - before, 0))
    through = jnp.cumsum(pair_count, axis=1)
    row_count = through[:, -1]
    positions = jnp.arange(KMAX)
    source = jnp.sum((through[:, None, :] <= positions[None, :, None]).astype(jnp.int32), axis=2)
    source = jnp.where(positions[None, :] < row_count[:, None], source, 0)
    return (source.astype(jnp.int32), row_count.astype(jnp.int32))


def draw_term_source(key, part):
    return term_tables(key)[0]


def draw_term_count(key, part):
    return term_tables(key)[1]


def with_ends(entries, own_key, least, high):
    longest = entries.shape.index(max(entries.shape))
    spots = []
    for shift in (0, 1):
        where = [jax.random.randint(jax.random.fold_in(own_key, axis), (), 0, length) for axis, length in enumerate(entries.shape)]
        where[longest] = (where[longest] + shift) % entries.shape[longest]
        spots.append(tuple(where))
    return entries.at[spots[0]].set(least).at[spots[1]].set(high)


def block_scale(rng, shape, cuts, low, largest):
    loudness, own = 1.0, jax.random.fold_in(rng, 6)
    for axis_at, shards_of in cuts:
        heights = jnp.exp(jax.random.uniform(jax.random.fold_in(own, axis_at), (shards_of,), jnp.float32, low / len(cuts), largest / len(cuts)))
        loudness = loudness * jnp.repeat(heights, shape[axis_at] // shards_of).reshape([-1 if axis == axis_at else 1 for axis in range(len(shape))])
    return loudness


def gaussian(own_key, extent, width, most, cuts=(), kind=jnp.bfloat16):
    result = width * jax.random.normal(own_key, extent, jnp.float32)
    if cuts:
        result = result * block_scale(own_key, extent, cuts, -0.22, 0.18)
    return jnp.clip(result, -most, most).astype(kind)


def setup_inputs(seed: int = 0) -> dict:
    keys = jax.random.split(jax.random.key(seed), 10)
    latlon = gaussian(keys[0], (BATCH, SOURCE_BLOCKS, SEG, CH), 1.0, 6.0, ((1, 8), (3, 4)))
    remap_weights = gaussian(keys[1], (N_TILE, EXT_CELLS, TERM_PTS), (TERM_PTS // 2) ** -0.5, 0.1875, ((0, 8),))
    term_source = draw_term_source(jax.random.fold_in(keys[9], 71), 0)
    term_block = with_ends(jax.random.randint(keys[3], (N_TILE, KMAX), 0, SRC_DEV), jax.random.fold_in(keys[3], 1), 0, SRC_DEV - 1).astype(jnp.int32)
    term_count = draw_term_count(jax.random.fold_in(keys[9], 71), 0)
    rotation = with_ends(jax.random.randint(keys[5], (N_TILE,), 0, 4), jax.random.fold_in(keys[5], 1), 0, 3).astype(jnp.int32)
    depthwise = gaussian(keys[6], (3, 3, CH), 9 ** -0.5, 2.0, ((2, 4),))
    pointwise = gaussian(keys[7], (CH, CH), CH ** -0.5, 0.25)
    cotangent = gaussian(keys[8], (BATCH, TOTAL_CELLS, CH), 1.0, 6.0, ((1, 8), (2, 4)))
    return dict(latlon=latlon, remap_weights=remap_weights, term_source=term_source, term_block=term_block, term_count=term_count, rotation=rotation, depthwise=depthwise, pointwise=pointwise, cotangent=cotangent)


def turn_kernel(kernel, turn, direction):
    turned = jnp.zeros_like(kernel)
    for quarter in range(4):
        turned = turned + jnp.where(turn == quarter, jnp.rot90(kernel, direction * quarter, axes=(0, 1)), 0.0)
    return turned


def stencil_apply(field, kernel):
    shape_out = (field.shape[0], TILE_EDGE, TILE_EDGE, field.shape[3])
    hidden = jnp.zeros(shape_out, jnp.float32)
    for row_off in range(3):
        for col_off in range(3):
            window = field[:, row_off:row_off + TILE_EDGE, col_off:col_off + TILE_EDGE, :].astype(jnp.float32)
            hidden = hidden + kernel[row_off, col_off] * window
    return hidden


def stencil_grads(field, kernel, grad_hidden):
    tap_rows = []
    grad_field = jnp.zeros(field.shape, jnp.float32)
    for row_off in range(3):
        tap_cols = []
        for col_off in range(3):
            window = field[:, row_off:row_off + TILE_EDGE, col_off:col_off + TILE_EDGE, :].astype(jnp.float32)
            tap_cols.append(jnp.sum(window * grad_hidden, axis=(0, 1, 2)))
            spread = kernel[row_off, col_off] * grad_hidden
            grad_field = grad_field + jnp.pad(spread, ((0, 0), (row_off, 2 - row_off), (col_off, 2 - col_off), (0, 0)))
        tap_rows.append(jnp.stack(tap_cols))
    return jnp.stack(tap_rows), grad_field


def reference(latlon, remap_weights, term_source, term_block, term_count, rotation, depthwise, pointwise, cotangent):
    kernel = depthwise.astype(jnp.float32)
    positions = jnp.arange(KMAX, dtype=jnp.int32)

    def one_tile(carry, tile_id):
        kernel_sum, mix_sum = carry
        in_use = positions < term_count[tile_id]
        block_index = (term_source[tile_id] * SRC_DEV + term_block[tile_id]).astype(jnp.int32)
        gathered = jnp.take(latlon, block_index, axis=1)
        gathered = jnp.where(in_use[None, :, None, None], gathered, jnp.zeros((), latlon.dtype))
        gathered = gathered.reshape(BATCH, TERM_PTS, CH)
        weights = remap_weights[tile_id].astype(jnp.float32)
        remapped = jnp.einsum("pk,bkc->bpc", weights, gathered.astype(jnp.float32)).astype(jnp.bfloat16)
        field = remapped.reshape(BATCH, TILE_EDGE + 2, TILE_EDGE + 2, CH)
        turned = turn_kernel(kernel, rotation[tile_id], 1)
        hidden = stencil_apply(field, turned)
        active = jax.nn.silu(hidden).astype(jnp.bfloat16).reshape(BATCH * TILE_CELLS, CH)
        mixed = jnp.dot(active, pointwise, preferred_element_type=jnp.float32).astype(jnp.bfloat16)
        upstream = lax.dynamic_slice_in_dim(cotangent, tile_id * TILE_CELLS, TILE_CELLS, 1)
        upstream = upstream.reshape(BATCH * TILE_CELLS, CH)
        grad_active = jnp.dot(upstream, pointwise.T, preferred_element_type=jnp.float32)
        sigma = jax.nn.sigmoid(hidden)
        grad_hidden = grad_active.reshape(hidden.shape) * sigma * (1.0 + hidden * (1.0 - sigma))
        grad_mix = jnp.dot(active.T, upstream, preferred_element_type=jnp.float32)
        grad_turned, grad_field = stencil_grads(field, turned, grad_hidden)
        grad_kernel = turn_kernel(grad_turned, rotation[tile_id], -1)
        grad_field = grad_field.astype(jnp.bfloat16).reshape(BATCH, EXT_CELLS, CH)
        grad_terms = jnp.einsum("pk,bpc->bkc", weights, grad_field.astype(jnp.float32))
        grad_terms = grad_terms.reshape(BATCH, KMAX, SEG, CH)
        grad_terms = jnp.where(in_use[None, :, None, None], grad_terms, 0.0).astype(jnp.bfloat16)
        outputs = (mixed.reshape(BATCH, TILE_CELLS, CH), grad_terms, block_index)
        return (kernel_sum + grad_kernel, mix_sum + grad_mix), outputs

    start_carry = (jnp.zeros((3, 3, CH), jnp.float32), jnp.zeros((CH, CH), jnp.float32))
    sums, stacked = lax.scan(one_tile, start_carry, jnp.arange(N_TILE, dtype=jnp.int32))
    kernel_sum, mix_sum = sums
    mixed_all, terms_all, blocks_all = stacked
    coupled = jnp.transpose(mixed_all, (1, 0, 2, 3)).reshape(BATCH, TOTAL_CELLS, CH)
    terms_flat = jnp.transpose(terms_all, (1, 0, 2, 3, 4)).reshape(BATCH, N_TILE * KMAX, SEG, CH)
    grad_latlon = jnp.zeros((BATCH, SOURCE_BLOCKS, SEG, CH), jnp.float32)
    grad_latlon = grad_latlon.at[:, blocks_all.reshape(-1)].add(terms_flat.astype(jnp.float32))
    factor = 1.0 / (CELLS ** 0.5)
    return coupled, grad_latlon.astype(jnp.bfloat16), kernel_sum * factor, mix_sum * factor
```

```python
import math

import jax
import jax.numpy as jnp
from jax import lax
from jax.sharding import PartitionSpec as P

TILE_EDGE = 32


def turn_kernel(kernel, turn, direction):
    turned = jnp.zeros_like(kernel)
    for quarter in range(4):
        turned = turned + jnp.where(
            turn == quarter, jnp.rot90(kernel, direction * quarter, axes=(0, 1)), 0.0
        )
    return turned


def stencil_apply(field, kernel):
    shape_out = (field.shape[0], TILE_EDGE, TILE_EDGE, field.shape[3])
    hidden = jnp.zeros(shape_out, jnp.float32)
    for row_off in range(3):
        for col_off in range(3):
            window = field[
                :, row_off : row_off + TILE_EDGE, col_off : col_off + TILE_EDGE, :
            ].astype(jnp.float32)
            hidden = hidden + kernel[row_off, col_off] * window
    return hidden


def stencil_grads(field, kernel, grad_hidden):
    tap_rows = []
    grad_field = jnp.zeros(field.shape, jnp.float32)
    for row_off in range(3):
        tap_cols = []
        for col_off in range(3):
            window = field[
                :, row_off : row_off + TILE_EDGE, col_off : col_off + TILE_EDGE, :
            ].astype(jnp.float32)
            tap_cols.append(jnp.sum(window * grad_hidden, axis=(0, 1, 2)))
            spread = kernel[row_off, col_off] * grad_hidden
            grad_field = grad_field + jnp.pad(
                spread, ((0, 0), (row_off, 2 - row_off), (col_off, 2 - col_off), (0, 0))
            )
        tap_rows.append(jnp.stack(tap_cols))
    return (jnp.stack(tap_rows), grad_field)


def every_chan(block):
    total = lax.axis_size("chan")
    copies = jnp.broadcast_to(block[None], (total, *block.shape))
    met = lax.all_to_all(copies, "chan", split_axis=0, concat_axis=0, tiled=True)
    return jnp.concatenate([met[i] for i in range(total)], axis=1)


def body(
    latlon,
    remap_weights,
    term_source,
    term_block,
    term_count,
    rotation,
    depthwise,
    pointwise,
    cotangent,
):
    tile_now = lax.axis_index("tile")
    tile_total = lax.axis_size("tile")
    chan_now = lax.axis_index("chan")
    batch_rows, block_total, seg_len, chan_local = latlon.shape
    terms_max = term_source.shape[1]
    capacity = 3 * terms_max // (2 * tile_total)
    ext_edge = TILE_EDGE + 2
    tile_cells = TILE_EDGE * TILE_EDGE
    flat_rows = batch_rows * tile_cells
    positions = jnp.arange(terms_max, dtype=jnp.int32)
    in_use = positions[None, :] < term_count[:, None]
    mine = in_use & (term_source == tile_now)
    before = (positions[:, None] <= positions[None, :]).astype(jnp.bfloat16)
    send_rank = jnp.dot(mine.astype(jnp.bfloat16), before, preferred_element_type=jnp.float32)
    send_rank = send_rank.astype(jnp.int32) - 1
    slot_ids = jnp.arange(capacity, dtype=jnp.int32)
    slot_hits = mine[:, None, :] & (send_rank[:, None, :] == slot_ids[None, :, None])
    slot_block = (jnp.sum(jnp.where(slot_hits, term_block[:, None, :] + 1, 0), axis=2) - 1).reshape(-1)
    blocks = jnp.arange(block_total, dtype=jnp.int32)
    send_pick = (slot_block[:, None] == blocks[None, :]).astype(jnp.bfloat16)
    outgoing = jnp.einsum("nb,abkc->ankc", send_pick, latlon, preferred_element_type=jnp.float32)
    outgoing = outgoing.astype(jnp.bfloat16)
    tile_mask = (jnp.arange(tile_total) == tile_now)[:, None]
    own_source = jnp.sum(jnp.where(tile_mask, term_source, 0), axis=0)
    own_count = jnp.sum(jnp.where(tile_mask[:, 0], term_count, 0))
    own_use = positions < own_count
    same_source = (
        (own_source[None, :] == own_source[:, None])
        & own_use[None, :]
        & (positions[None, :] <= positions[:, None])
    )
    own_rank = jnp.sum(same_source.astype(jnp.int32), axis=1) - 1
    recv_slot = jnp.where(own_use, own_source * capacity + own_rank, -1)
    slots = jnp.arange(tile_total * capacity, dtype=jnp.int32)
    recv_pick = (recv_slot[:, None] == slots[None, :]).astype(jnp.bfloat16)
    weights = remap_weights[0]
    ext_cells = weights.shape[0]
    term_pts = weights.shape[1]
    arrived = lax.all_to_all(outgoing, "tile", split_axis=1, concat_axis=1, tiled=True)
    picked = jnp.einsum("tn,ankc->atkc", recv_pick, arrived, preferred_element_type=jnp.float32)
    picked = picked.astype(jnp.bfloat16)
    picked = picked.reshape(picked.shape[0], term_pts, chan_local)
    mapped = jnp.einsum("pk,bkc->bpc", weights, picked, preferred_element_type=jnp.float32)
    remapped = mapped.astype(jnp.bfloat16)
    field = remapped.reshape(batch_rows, ext_edge, ext_edge, chan_local)
    turn = rotation[0]
    kernel = turn_kernel(depthwise.astype(jnp.float32), turn, 1)
    hidden = stencil_apply(field, kernel)
    active = jax.nn.silu(hidden).astype(jnp.bfloat16).reshape(flat_rows, chan_local)
    own_rows = lax.dynamic_slice_in_dim(pointwise, chan_now * chan_local, chan_local, 0)
    own_cols = lax.dynamic_slice_in_dim(pointwise, chan_now * chan_local, chan_local, 1)
    mixed = jnp.dot(every_chan(active), own_cols, preferred_element_type=jnp.float32)
    coupled = mixed.astype(jnp.bfloat16).reshape(batch_rows, tile_cells, chan_local)
    upstream = cotangent.reshape(flat_rows, chan_local)
    piece = every_chan(upstream)
    grad_active = lax.dot_general(
        piece, own_rows, (((1,), (1,)), ((), ())), preferred_element_type=jnp.float32
    )
    block_grad = lax.dot_general(
        active, piece, (((0,), (0,)), ((), ())), preferred_element_type=jnp.float32
    )
    grad_mix = block_grad
    grad_active, grad_mix = (grad_active, grad_mix)
    sigma = jax.nn.sigmoid(hidden)
    grad_hidden = grad_active.reshape(hidden.shape) * sigma * (1.0 + hidden * (1.0 - sigma))
    grad_turned, grad_field = stencil_grads(field, kernel, grad_hidden)
    grad_field = grad_field.astype(jnp.bfloat16).reshape(batch_rows, ext_cells, chan_local)
    grad_terms = jnp.einsum("pk,bpc->bkc", weights, grad_field, preferred_element_type=jnp.float32)
    grad_terms = grad_terms.astype(jnp.bfloat16).reshape(batch_rows, terms_max, seg_len, chan_local)
    returning = jnp.einsum("tn,atkc->ankc", recv_pick, grad_terms, preferred_element_type=jnp.float32)
    returning = returning.astype(jnp.bfloat16)
    arrived = lax.all_to_all(returning, "tile", split_axis=1, concat_axis=1, tiled=True)
    summed = jnp.einsum("nb,ankc->abkc", send_pick, arrived, preferred_element_type=jnp.float32)
    grad_latlon = summed.astype(jnp.bfloat16)
    grad_kernel = turn_kernel(grad_turned, turn, -1)
    kernel_sum, mix_sum = lax.psum((grad_kernel, grad_mix), "tile")
    factor = 1.0 / math.sqrt(batch_rows * tile_cells * tile_total)
    return (coupled, grad_latlon, kernel_sum * factor, mix_sum * factor)


def solution(mesh):
    return jax.shard_map(
        body,
        mesh=mesh,
        in_specs=(
            P(None, "tile", None, "chan"),
            P("tile", None, None),
            P(),
            P(),
            P(),
            P("tile"),
            P(None, None, "chan"),
            P(),
            P(None, "tile", "chan"),
        ),
        out_specs=(
            P(None, "tile", "chan"),
            P(None, "tile", None, "chan"),
            P(None, None, "chan"),
            P("chan", None),
        ),
        check_vma=False,
    )
```

```python
import math

import jax
import jax.numpy as jnp
from jax import lax
from jax.experimental import pallas as pl
from jax.experimental.pallas import tpu as pltpu
from jax.sharding import PartitionSpec as P

TILE_EDGE = 32


def turn_kernel(kernel, turn, direction):
    turned = jnp.zeros_like(kernel)
    for quarter in range(4):
        turned = turned + jnp.where(
            turn == quarter, jnp.rot90(kernel, direction * quarter, axes=(0, 1)), 0.0
        )
    return turned


def stencil_apply(field, kernel):
    shape_out = (field.shape[0], TILE_EDGE, TILE_EDGE, field.shape[3])
    hidden = jnp.zeros(shape_out, jnp.float32)
    for row_off in range(3):
        for col_off in range(3):
            window = field[
                :, row_off : row_off + TILE_EDGE, col_off : col_off + TILE_EDGE, :
            ].astype(jnp.float32)
            hidden = hidden + kernel[row_off, col_off] * window
    return hidden


def stencil_grads(field, kernel, grad_hidden):
    tap_rows = []
    grad_field = jnp.zeros(field.shape, jnp.float32)
    for row_off in range(3):
        tap_cols = []
        for col_off in range(3):
            window = field[
                :, row_off : row_off + TILE_EDGE, col_off : col_off + TILE_EDGE, :
            ].astype(jnp.float32)
            tap_cols.append(jnp.sum(window * grad_hidden, axis=(0, 1, 2)))
            spread = kernel[row_off, col_off] * grad_hidden
            grad_field = grad_field + jnp.pad(
                spread, ((0, 0), (row_off, 2 - row_off), (col_off, 2 - col_off), (0, 0))
            )
        tap_rows.append(jnp.stack(tap_cols))
    return (jnp.stack(tap_rows), grad_field)


CHUNKS = 4


def greet():
    barrier = pltpu.get_barrier_semaphore()
    met = 0
    for axis in ("tile", "chan"):
        total, here = lax.axis_size(axis), lax.axis_index(axis)
        for step in range(1, total):
            pl.semaphore_signal(
                barrier,
                inc=1,
                device_id={axis: lax.rem(here + step, total)},
                device_id_type=pl.DeviceIdType.MESH,
            )
            met += 1
    pl.semaphore_wait(barrier, met)


def send(src, dst, sems, place, where):
    copy = pltpu.make_async_remote_copy(
        src_ref=src,
        dst_ref=dst,
        send_sem=sems.at[(0, *place)],
        recv_sem=sems.at[(1, *place)],
        device_id=where,
        device_id_type=pl.DeviceIdType.MESH,
    )
    return copy


def swap_start(src, dst, rows, sems, spread):
    total, here = lax.axis_size("tile"), lax.axis_index("tile")
    into = pl.ds(pl.multiple_of(here * rows, rows), rows)
    own = src if spread else src.at[into]
    copies = [pltpu.make_async_copy(own, dst.at[into], sems.at[0, 0])]
    for step in range(1, total):
        peer = lax.rem(here + step, total)
        part = src if spread else src.at[pl.ds(pl.multiple_of(peer * rows, rows), rows)]
        copies.append(send(part, dst.at[into], sems, (step,), {"tile": peer}))
    for copy in copies:
        copy.start()
    return copies


def wait_all(copies):
    for copy in copies:
        copy.wait()


def line_gather(own, full, sems, local_sem, after=None):
    total, here = lax.axis_size("chan"), lax.axis_index("chan")
    wide, rows = own.shape[1], own.shape[0] // CHUNKS

    def at(ref, who, chunk):
        return ref.at[
            pl.ds(chunk * rows, rows), pl.ds(pl.multiple_of(who * wide, wide), wide)
        ]

    def hop(way, step, chunk):
        shift = 1 - 2 * way
        who = jnp.clip(here - shift * step, 0, total - 1)
        src = own.at[pl.ds(chunk * rows, rows)] if step == 0 else at(full, who, chunk)
        return send(
            src,
            at(full, who, chunk),
            sems,
            (way, step, chunk),
            {"chan": jnp.clip(here + shift, 0, total - 1)},
        )

    def far(way, step):
        return here >= step if way == 0 else here <= total - 1 - step

    def sends(way, step):
        return far(way, step) & (here < total - 1 if way == 0 else here > 0)

    local = pltpu.make_async_copy(
        own, full.at[:, pl.ds(pl.multiple_of(here * wide, wide), wide)], local_sem
    )
    local.start()
    for step in range(total):
        for chunk in range(CHUNKS):
            for way in range(2):
                if step > 0:

                    @pl.when(far(way, step))
                    def _(way=way, step=step, chunk=chunk):
                        hop(way, step - 1, chunk).wait_recv()

                if step < total - 1:

                    @pl.when(sends(way, step))
                    def _(way=way, step=step, chunk=chunk):
                        hop(way, step, chunk).start()

        if step == 1 and after is not None:
            after()
    for step in range(total - 1):
        for chunk in range(CHUNKS):
            for way in range(2):

                @pl.when(sends(way, step))
                def _(way=way, step=step, chunk=chunk):
                    hop(way, step, chunk).wait_send()

    local.wait()


def first_kernel(out_ref, own_ref, in_ref, full_ref, swap_sems, line_sems, local_sem):
    greet()
    rows = out_ref.shape[0] // lax.axis_size("tile")
    copies = swap_start(out_ref, in_ref, rows, swap_sems, False)
    line_gather(own_ref, full_ref, line_sems, local_sem)
    wait_all(copies)


def second_kernel(
    out_ref,
    own_ref,
    mix_ref,
    taps_ref,
    in_ref,
    full_ref,
    mix_out,
    taps_out,
    mix_parts,
    mix_own,
    taps_parts,
    swap_sems,
    line_sems,
    mix_sems,
    back_sems,
    taps_sems,
    local_sem,
):
    greet()
    total = lax.axis_size("tile")
    mix_rows = mix_ref.shape[0] // total
    mix_copies = swap_start(mix_ref, mix_parts, mix_rows, mix_sems, False)
    taps_copies = swap_start(taps_ref, taps_parts, taps_ref.shape[0], taps_sems, True)
    copies = swap_start(out_ref, in_ref, out_ref.shape[0] // total, swap_sems, False)
    back = []

    def reduce():
        wait_all(mix_copies)
        summed = mix_parts[0:mix_rows]
        for part in range(1, total):
            summed = summed + mix_parts[part * mix_rows : (part + 1) * mix_rows]
        mix_own[...] = summed.astype(mix_own.dtype)
        back.extend(swap_start(mix_own, mix_out, mix_rows, back_sems, True))

    line_gather(own_ref, full_ref, line_sems, local_sem, reduce)
    wait_all(taps_copies)
    tap_rows = taps_ref.shape[0]
    taps = taps_parts[0:tap_rows]
    for part in range(1, total):
        taps = taps + taps_parts[part * tap_rows : (part + 1) * tap_rows]
    taps_out[...] = taps
    wait_all(back)
    wait_all(copies)


def call(kernel, shapes, scratch, sems, collective_id, *operands):
    vmem = pl.BlockSpec(memory_space=pltpu.VMEM)
    line = (2, 2, lax.axis_size("chan"), CHUNKS)
    return pl.pallas_call(
        kernel,
        out_shape=[jax.ShapeDtypeStruct(*one) for one in shapes],
        in_specs=[vmem] * len(operands),
        out_specs=[vmem] * len(shapes),
        scratch_shapes=[
            *[pltpu.VMEM(*one) for one in scratch],
            pltpu.SemaphoreType.DMA((2, lax.axis_size("tile"))),
            pltpu.SemaphoreType.DMA(line),
            *[pltpu.SemaphoreType.DMA((2, lax.axis_size("tile")))] * sems,
            pltpu.SemaphoreType.DMA,
        ],
        compiler_params=pltpu.CompilerParams(
            collective_id=collective_id,
            has_side_effects=True,
            vmem_limit_bytes=24 * 2**20,
        ),
    )(*operands)


def body(
    latlon,
    remap_weights,
    term_source,
    term_block,
    term_count,
    rotation,
    depthwise,
    pointwise,
    cotangent,
):
    tile_now = lax.axis_index("tile")
    tile_total = lax.axis_size("tile")
    chan_now = lax.axis_index("chan")
    batch_rows, block_total, seg_len, chan_local = latlon.shape
    terms_max = term_source.shape[1]
    capacity = 3 * terms_max // (2 * tile_total)
    ext_edge = TILE_EDGE + 2
    tile_cells = TILE_EDGE * TILE_EDGE
    flat_rows = batch_rows * tile_cells
    positions = jnp.arange(terms_max, dtype=jnp.int32)
    in_use = positions[None, :] < term_count[:, None]
    mine = in_use & (term_source == tile_now)
    before = (positions[:, None] <= positions[None, :]).astype(jnp.bfloat16)
    send_rank = jnp.dot(mine.astype(jnp.bfloat16), before, preferred_element_type=jnp.float32)
    send_rank = send_rank.astype(jnp.int32) - 1
    slot_ids = jnp.arange(capacity, dtype=jnp.int32)
    slot_hits = mine[:, None, :] & (send_rank[:, None, :] == slot_ids[None, :, None])
    slot_block = (jnp.sum(jnp.where(slot_hits, term_block[:, None, :] + 1, 0), axis=2) - 1).reshape(-1)
    blocks = jnp.arange(block_total, dtype=jnp.int32)
    send_pick = (slot_block[:, None] == blocks[None, :]).astype(jnp.bfloat16)
    outgoing = jnp.einsum("nb,abkc->ankc", send_pick, latlon, preferred_element_type=jnp.float32)
    outgoing = outgoing.astype(jnp.bfloat16)
    tile_mask = (jnp.arange(tile_total) == tile_now)[:, None]
    own_source = jnp.sum(jnp.where(tile_mask, term_source, 0), axis=0)
    own_count = jnp.sum(jnp.where(tile_mask[:, 0], term_count, 0))
    own_use = positions < own_count
    same_source = (
        (own_source[None, :] == own_source[:, None])
        & own_use[None, :]
        & (positions[None, :] <= positions[:, None])
    )
    own_rank = jnp.sum(same_source.astype(jnp.int32), axis=1) - 1
    recv_slot = jnp.where(own_use, own_source * capacity + own_rank, -1)
    slots = jnp.arange(tile_total * capacity, dtype=jnp.int32)
    recv_pick = (recv_slot[:, None] == slots[None, :]).astype(jnp.bfloat16)
    weights = remap_weights[0]
    ext_cells = weights.shape[0]
    term_pts = weights.shape[1]
    slot_shape = outgoing.shape
    upstream = cotangent.reshape(flat_rows, chan_local)
    chan_total = lax.axis_size("chan")
    outgoing = outgoing.reshape(-1, chan_local)
    whole_shape = (flat_rows, chan_total * chan_local)
    arrived, piece = call(
        first_kernel,
        ((outgoing.shape, jnp.bfloat16), (whole_shape, jnp.bfloat16)),
        (),
        0,
        0,
        outgoing,
        upstream,
    )
    arrived = arrived.reshape(slot_shape)
    picked = jnp.einsum("tn,ankc->atkc", recv_pick, arrived, preferred_element_type=jnp.float32)
    picked = picked.astype(jnp.bfloat16)
    picked = picked.reshape(picked.shape[0], term_pts, chan_local)
    mapped = jnp.einsum("pk,bkc->bpc", weights, picked, preferred_element_type=jnp.float32)
    remapped = mapped.astype(jnp.bfloat16)
    field = remapped.reshape(batch_rows, ext_edge, ext_edge, chan_local)
    turn = rotation[0]
    kernel = turn_kernel(depthwise.astype(jnp.float32), turn, 1)
    hidden = stencil_apply(field, kernel)
    active = jax.nn.silu(hidden).astype(jnp.bfloat16).reshape(flat_rows, chan_local)
    own_rows = lax.dynamic_slice_in_dim(pointwise, chan_now * chan_local, chan_local, 0)
    own_cols = lax.dynamic_slice_in_dim(pointwise, chan_now * chan_local, chan_local, 1)
    grad_active = lax.dot_general(
        piece, own_rows, (((1,), (1,)), ((), ())), preferred_element_type=jnp.float32
    )
    block_grad = lax.dot_general(
        active, piece, (((0,), (0,)), ((), ())), preferred_element_type=jnp.float32
    )
    grad_mix = block_grad
    grad_active, grad_mix = (grad_active, grad_mix)
    sigma = jax.nn.sigmoid(hidden)
    grad_hidden = grad_active.reshape(hidden.shape) * sigma * (1.0 + hidden * (1.0 - sigma))
    grad_turned, grad_field = stencil_grads(field, kernel, grad_hidden)
    grad_field = grad_field.astype(jnp.bfloat16).reshape(batch_rows, ext_cells, chan_local)
    grad_terms = jnp.einsum("pk,bpc->bkc", weights, grad_field, preferred_element_type=jnp.float32)
    grad_terms = grad_terms.astype(jnp.bfloat16).reshape(batch_rows, terms_max, seg_len, chan_local)
    returning = jnp.einsum("tn,atkc->ankc", recv_pick, grad_terms, preferred_element_type=jnp.float32)
    returning = returning.astype(jnp.bfloat16)
    grad_kernel = turn_kernel(grad_turned, turn, -1).reshape(9, chan_local)
    grad_kernel = jnp.pad(grad_kernel, ((0, 7), (0, 0)))
    grad_mix = jnp.concatenate(
        [grad_mix[:, i * chan_local : (i + 1) * chan_local] for i in range(chan_total)]
    )
    returning = returning.reshape(-1, chan_local)
    mix_rows = grad_mix.shape[0] // tile_total
    mix_type = jnp.bfloat16 if mix_rows % 16 == 0 else jnp.float32
    arrived, active_all, mix_sum, kernel_sum = call(
        second_kernel,
        (
            (returning.shape, jnp.bfloat16),
            (whole_shape, jnp.bfloat16),
            (grad_mix.shape, mix_type),
            (grad_kernel.shape, jnp.float32),
        ),
        (
            (grad_mix.shape, jnp.float32),
            ((mix_rows, chan_local), mix_type),
            ((tile_total * grad_kernel.shape[0], chan_local), jnp.float32),
        ),
        3,
        1,
        returning,
        active,
        grad_mix,
        grad_kernel,
    )
    mixed = jnp.dot(active_all, own_cols, preferred_element_type=jnp.float32)
    coupled = mixed.astype(jnp.bfloat16).reshape(batch_rows, tile_cells, chan_local)
    arrived = arrived.reshape(slot_shape)
    mix_sum = mix_sum.astype(jnp.float32)
    mix_sum = jnp.concatenate(
        [mix_sum[i * chan_local : (i + 1) * chan_local] for i in range(chan_total)], axis=1
    )
    kernel_sum = kernel_sum[:9].reshape(3, 3, chan_local)
    summed = jnp.einsum("nb,ankc->abkc", send_pick, arrived, preferred_element_type=jnp.float32)
    grad_latlon = summed.astype(jnp.bfloat16)
    factor = 1.0 / math.sqrt(batch_rows * tile_cells * tile_total)
    return (coupled, grad_latlon, kernel_sum * factor, mix_sum * factor)


def solution(mesh):
    return jax.shard_map(
        body,
        mesh=mesh,
        in_specs=(
            P(None, "tile", None, "chan"),
            P("tile", None, None),
            P(),
            P(),
            P(),
            P("tile"),
            P(None, None, "chan"),
            P(),
            P(None, "tile", "chan"),
        ),
        out_specs=(
            P(None, "tile", "chan"),
            P(None, "tile", None, "chan"),
            P(None, None, "chan"),
            P("chan", None),
        ),
        check_vma=False,
    )
```

```python
import math

import jax
import jax.numpy as jnp
from jax import lax
from jax.experimental import pallas as pl
from jax.experimental.pallas import tpu as pltpu
from jax.sharding import PartitionSpec as P

TILE_EDGE = 32


def turn_kernel(kernel, turn, direction):
    turned = jnp.zeros_like(kernel)
    for quarter in range(4):
        turned = turned + jnp.where(
            turn == quarter, jnp.rot90(kernel, direction * quarter, axes=(0, 1)), 0.0
        )
    return turned


def stencil_apply(field, kernel):
    shape_out = (field.shape[0], TILE_EDGE, TILE_EDGE, field.shape[3])
    hidden = jnp.zeros(shape_out, jnp.float32)
    for row_off in range(3):
        for col_off in range(3):
            window = field[
                :, row_off : row_off + TILE_EDGE, col_off : col_off + TILE_EDGE, :
            ].astype(jnp.float32)
            hidden = hidden + kernel[row_off, col_off] * window
    return hidden


def stencil_grads(field, kernel, grad_hidden):
    tap_rows = []
    grad_field = jnp.zeros(field.shape, jnp.float32)
    for row_off in range(3):
        tap_cols = []
        for col_off in range(3):
            window = field[
                :, row_off : row_off + TILE_EDGE, col_off : col_off + TILE_EDGE, :
            ].astype(jnp.float32)
            tap_cols.append(jnp.sum(window * grad_hidden, axis=(0, 1, 2)))
            spread = kernel[row_off, col_off] * grad_hidden
            grad_field = grad_field + jnp.pad(
                spread, ((0, 0), (row_off, 2 - row_off), (col_off, 2 - col_off), (0, 0))
            )
        tap_rows.append(jnp.stack(tap_cols))
    return (jnp.stack(tap_rows), grad_field)


CHUNKS = 4


def greet():
    barrier = pltpu.get_barrier_semaphore()
    met = 0
    for axis in ("tile", "chan"):
        total, here = lax.axis_size(axis), lax.axis_index(axis)
        for step in range(1, total):
            pl.semaphore_signal(
                barrier,
                inc=1,
                device_id={axis: lax.rem(here + step, total)},
                device_id_type=pl.DeviceIdType.MESH,
            )
            met += 1
    pl.semaphore_wait(barrier, met)


def send(src, dst, sems, place, where):
    copy = pltpu.make_async_remote_copy(
        src_ref=src,
        dst_ref=dst,
        send_sem=sems.at[(0, *place)],
        recv_sem=sems.at[(1, *place)],
        device_id=where,
        device_id_type=pl.DeviceIdType.MESH,
    )
    return copy


def swap_start(src, dst, rows, sems, spread):
    total, here = lax.axis_size("tile"), lax.axis_index("tile")
    into = pl.ds(pl.multiple_of(here * rows, rows), rows)
    own = src if spread else src.at[into]
    copies = [pltpu.make_async_copy(own, dst.at[into], sems.at[0, 0])]
    for step in range(1, total):
        peer = lax.rem(here + step, total)
        part = src if spread else src.at[pl.ds(pl.multiple_of(peer * rows, rows), rows)]
        copies.append(send(part, dst.at[into], sems, (step,), {"tile": peer}))
    for copy in copies:
        copy.start()
    return copies


def wait_all(copies):
    for copy in copies:
        copy.wait()


def line_gather(own, full, sems, local_sem, between):
    total, here = lax.axis_size("chan"), lax.axis_index("chan")
    wide, rows = own.shape[1], own.shape[0] // CHUNKS

    def at(ref, who, chunk):
        return ref.at[
            pl.ds(chunk * rows, rows), pl.ds(pl.multiple_of(who * wide, wide), wide)
        ]

    def hop(way, step, chunk):
        shift = 1 - 2 * way
        who = jnp.clip(here - shift * step, 0, total - 1)
        src = own.at[pl.ds(chunk * rows, rows)] if step == 0 else at(full, who, chunk)
        return send(
            src,
            at(full, who, chunk),
            sems,
            (way, step, chunk),
            {"chan": jnp.clip(here + shift, 0, total - 1)},
        )

    def far(way, step):
        return here >= step if way == 0 else here <= total - 1 - step

    def sends(way, step):
        return far(way, step) & (here < total - 1 if way == 0 else here > 0)

    local = pltpu.make_async_copy(
        own, full.at[:, pl.ds(pl.multiple_of(here * wide, wide), wide)], local_sem
    )
    local.start()
    for step in range(total):
        for chunk in range(CHUNKS):
            for way in range(2):
                if step > 0:

                    @pl.when(far(way, step))
                    def _(way=way, step=step, chunk=chunk):
                        hop(way, step - 1, chunk).wait_recv()

                if step < total - 1:

                    @pl.when(sends(way, step))
                    def _(way=way, step=step, chunk=chunk):
                        hop(way, step, chunk).start()

        if step in between:
            between[step]()
    for step in range(total - 1):
        for chunk in range(CHUNKS):
            for way in range(2):

                @pl.when(sends(way, step))
                def _(way=way, step=step, chunk=chunk):
                    hop(way, step, chunk).wait_send()

    local.wait()


def first_kernel(
    out_ref,
    own_ref,
    pick_ref,
    weights_ref,
    in_ref,
    full_ref,
    mapped_ref,
    weights,
    slots,
    picked,
    swap_sems,
    line_sems,
    local_sem,
    weights_sem,
):
    fetch = pltpu.make_async_copy(weights_ref, weights, weights_sem)
    fetch.start()
    greet()
    rows = out_ref.shape[0] // lax.axis_size("tile")
    copies = swap_start(out_ref, in_ref, rows, swap_sems, False)
    terms, filled = pick_ref.shape
    seg = out_ref.shape[0] // filled

    def remap():
        wait_all(copies)
        slots[...] = in_ref[...].astype(jnp.float32)
        for point in range(seg):
            part = slots[pl.ds(point, filled, stride=seg), :].astype(jnp.bfloat16)
            picked[pl.ds(point, terms, stride=seg), :] = jnp.dot(
                pick_ref[...], part, preferred_element_type=jnp.float32
            )
        fetch.wait()
        mapped_ref[...] = jnp.dot(
            weights[...],
            picked[...].astype(jnp.bfloat16),
            preferred_element_type=jnp.float32,
        ).astype(jnp.bfloat16)

    last = lax.axis_size("chan") - 2
    line_gather(own_ref, full_ref, line_sems, local_sem, {last: remap})


def second_kernel(
    grad_ref,
    own_ref,
    pick_ref,
    weights_ref,
    mix_ref,
    taps_ref,
    in_ref,
    full_ref,
    mix_out,
    taps_out,
    mix_parts,
    mix_own,
    taps_parts,
    weights,
    terms_ref,
    slots,
    out_ref,
    swap_sems,
    line_sems,
    mix_sems,
    back_sems,
    taps_sems,
    local_sem,
    weights_sem,
):
    fetch = pltpu.make_async_copy(weights_ref, weights, weights_sem)
    fetch.start()
    greet()
    total = lax.axis_size("tile")
    mix_rows = mix_ref.shape[0] // total
    mix_copies = swap_start(mix_ref, mix_parts, mix_rows, mix_sems, False)
    taps_copies = swap_start(taps_ref, taps_parts, taps_ref.shape[0], taps_sems, True)
    copies, back = [], []
    terms, filled = pick_ref.shape
    seg = out_ref.shape[0] // filled

    def unmap():
        fetch.wait()
        turned = lax.dot_general(
            grad_ref[...],
            weights[...],
            (((0,), (0,)), ((), ())),
            preferred_element_type=jnp.float32,
        )
        terms_ref[...] = turned.T
        for point in range(seg):
            part = terms_ref[pl.ds(point, terms, stride=seg), :].astype(jnp.bfloat16)
            slots[pl.ds(point, filled, stride=seg), :] = lax.dot_general(
                pick_ref[...],
                part,
                (((0,), (0,)), ((), ())),
                preferred_element_type=jnp.float32,
            )
        out_ref[...] = slots[...].astype(jnp.bfloat16)
        rows = out_ref.shape[0] // total
        copies.extend(swap_start(out_ref, in_ref, rows, swap_sems, False))

    def reduce():
        wait_all(mix_copies)
        summed = mix_parts[0:mix_rows]
        for part in range(1, total):
            summed = summed + mix_parts[part * mix_rows : (part + 1) * mix_rows]
        mix_own[...] = summed.astype(mix_own.dtype)
        back.extend(swap_start(mix_own, mix_out, mix_rows, back_sems, True))

    line_gather(own_ref, full_ref, line_sems, local_sem, {0: unmap, 1: reduce})
    wait_all(taps_copies)
    tap_rows = taps_ref.shape[0]
    taps = taps_parts[0:tap_rows]
    for part in range(1, total):
        taps = taps + taps_parts[part * tap_rows : (part + 1) * tap_rows]
    taps_out[...] = taps
    wait_all(back)
    wait_all(copies)


def call(kernel, shapes, scratch, sems, collective_id, *operands):
    vmem = pl.BlockSpec(memory_space=pltpu.VMEM)
    line = (2, 2, lax.axis_size("chan"), CHUNKS)
    return pl.pallas_call(
        kernel,
        out_shape=[jax.ShapeDtypeStruct(*one) for one in shapes],
        in_specs=[
            pl.BlockSpec(memory_space=pl.ANY) if at == 3 else vmem
            for at in range(len(operands))
        ],
        out_specs=[vmem] * len(shapes),
        scratch_shapes=[
            *[pltpu.VMEM(*one) for one in scratch],
            pltpu.SemaphoreType.DMA((2, lax.axis_size("tile"))),
            pltpu.SemaphoreType.DMA(line),
            *[pltpu.SemaphoreType.DMA((2, lax.axis_size("tile")))] * sems,
            pltpu.SemaphoreType.DMA,
            pltpu.SemaphoreType.DMA,
        ],
        compiler_params=pltpu.CompilerParams(
            collective_id=collective_id,
            has_side_effects=True,
            vmem_limit_bytes=40 * 2**20,
        ),
    )(*operands)


def body(
    latlon,
    remap_weights,
    term_source,
    term_block,
    term_count,
    rotation,
    depthwise,
    pointwise,
    cotangent,
):
    tile_now = lax.axis_index("tile")
    tile_total = lax.axis_size("tile")
    chan_now = lax.axis_index("chan")
    batch_rows, block_total, seg_len, chan_local = latlon.shape
    terms_max = term_source.shape[1]
    capacity = 3 * terms_max // (2 * tile_total)
    ext_edge = TILE_EDGE + 2
    tile_cells = TILE_EDGE * TILE_EDGE
    flat_rows = batch_rows * tile_cells
    positions = jnp.arange(terms_max, dtype=jnp.int32)
    in_use = positions[None, :] < term_count[:, None]
    mine = in_use & (term_source == tile_now)
    before = (positions[:, None] <= positions[None, :]).astype(jnp.bfloat16)
    send_rank = jnp.dot(mine.astype(jnp.bfloat16), before, preferred_element_type=jnp.float32)
    send_rank = send_rank.astype(jnp.int32) - 1
    slot_ids = jnp.arange(capacity, dtype=jnp.int32)
    slot_hits = mine[:, None, :] & (send_rank[:, None, :] == slot_ids[None, :, None])
    slot_block = (jnp.sum(jnp.where(slot_hits, term_block[:, None, :] + 1, 0), axis=2) - 1).reshape(-1)
    blocks = jnp.arange(block_total, dtype=jnp.int32)
    send_pick = (slot_block[:, None] == blocks[None, :]).astype(jnp.bfloat16)
    outgoing = jnp.einsum("nb,abkc->ankc", send_pick, latlon, preferred_element_type=jnp.float32)
    outgoing = outgoing.astype(jnp.bfloat16)
    tile_mask = (jnp.arange(tile_total) == tile_now)[:, None]
    own_source = jnp.sum(jnp.where(tile_mask, term_source, 0), axis=0)
    own_count = jnp.sum(jnp.where(tile_mask[:, 0], term_count, 0))
    own_use = positions < own_count
    same_source = (
        (own_source[None, :] == own_source[:, None])
        & own_use[None, :]
        & (positions[None, :] <= positions[:, None])
    )
    own_rank = jnp.sum(same_source.astype(jnp.int32), axis=1) - 1
    recv_slot = jnp.where(own_use, own_source * capacity + own_rank, -1)
    slots = jnp.arange(tile_total * capacity, dtype=jnp.int32)
    recv_pick = (recv_slot[:, None] == slots[None, :]).astype(jnp.bfloat16)
    weights = remap_weights[0]
    ext_cells = weights.shape[0]
    term_pts = weights.shape[1]
    slot_shape = outgoing.shape
    upstream = cotangent.reshape(flat_rows, chan_local)
    chan_total = lax.axis_size("chan")
    outgoing = outgoing.reshape(-1, chan_local)
    whole_shape = (flat_rows, chan_total * chan_local)
    points = (term_pts, chan_local)
    _, piece, remapped = call(
        first_kernel,
        (
            (outgoing.shape, jnp.bfloat16),
            (whole_shape, jnp.bfloat16),
            ((ext_cells, chan_local), jnp.bfloat16),
        ),
        (
            (weights.shape, jnp.bfloat16),
            (outgoing.shape, jnp.float32),
            (points, jnp.float32),
        ),
        0,
        0,
        outgoing,
        upstream,
        recv_pick,
        weights,
    )
    field = remapped.reshape(batch_rows, ext_edge, ext_edge, chan_local)
    turn = rotation[0]
    kernel = turn_kernel(depthwise.astype(jnp.float32), turn, 1)
    hidden = stencil_apply(field, kernel)
    active = jax.nn.silu(hidden).astype(jnp.bfloat16).reshape(flat_rows, chan_local)
    own_rows = lax.dynamic_slice_in_dim(pointwise, chan_now * chan_local, chan_local, 0)
    own_cols = lax.dynamic_slice_in_dim(pointwise, chan_now * chan_local, chan_local, 1)
    grad_active = lax.dot_general(
        piece, own_rows, (((1,), (1,)), ((), ())), preferred_element_type=jnp.float32
    )
    block_grad = lax.dot_general(
        active, piece, (((0,), (0,)), ((), ())), preferred_element_type=jnp.float32
    )
    grad_mix = block_grad
    grad_active, grad_mix = (grad_active, grad_mix)
    sigma = jax.nn.sigmoid(hidden)
    grad_hidden = grad_active.reshape(hidden.shape) * sigma * (1.0 + hidden * (1.0 - sigma))
    grad_turned, grad_field = stencil_grads(field, kernel, grad_hidden)
    grad_field = grad_field.astype(jnp.bfloat16).reshape(ext_cells, chan_local)
    grad_kernel = turn_kernel(grad_turned, turn, -1).reshape(9, chan_local)
    grad_kernel = jnp.pad(grad_kernel, ((0, 7), (0, 0)))
    grad_mix = jnp.concatenate(
        [grad_mix[:, i * chan_local : (i + 1) * chan_local] for i in range(chan_total)]
    )
    mix_rows = grad_mix.shape[0] // tile_total
    mix_type = jnp.bfloat16 if mix_rows % 16 == 0 else jnp.float32
    arrived, active_all, mix_sum, kernel_sum = call(
        second_kernel,
        (
            (outgoing.shape, jnp.bfloat16),
            (whole_shape, jnp.bfloat16),
            (grad_mix.shape, mix_type),
            (grad_kernel.shape, jnp.float32),
        ),
        (
            (grad_mix.shape, jnp.float32),
            ((mix_rows, chan_local), mix_type),
            ((tile_total * grad_kernel.shape[0], chan_local), jnp.float32),
            (weights.shape, jnp.bfloat16),
            (points, jnp.float32),
            (outgoing.shape, jnp.float32),
            (outgoing.shape, jnp.bfloat16),
        ),
        3,
        1,
        grad_field,
        active,
        recv_pick,
        weights,
        grad_mix,
        grad_kernel,
    )
    mixed = jnp.dot(active_all, own_cols, preferred_element_type=jnp.float32)
    coupled = mixed.astype(jnp.bfloat16).reshape(batch_rows, tile_cells, chan_local)
    arrived = arrived.reshape(slot_shape)
    mix_sum = mix_sum.astype(jnp.float32)
    mix_sum = jnp.concatenate(
        [mix_sum[i * chan_local : (i + 1) * chan_local] for i in range(chan_total)], axis=1
    )
    kernel_sum = kernel_sum[:9].reshape(3, 3, chan_local)
    summed = jnp.einsum("nb,ankc->abkc", send_pick, arrived, preferred_element_type=jnp.float32)
    grad_latlon = summed.astype(jnp.bfloat16)
    factor = 1.0 / math.sqrt(batch_rows * tile_cells * tile_total)
    return (coupled, grad_latlon, kernel_sum * factor, mix_sum * factor)


def solution(mesh):
    return jax.shard_map(
        body,
        mesh=mesh,
        in_specs=(
            P(None, "tile", None, "chan"),
            P("tile", None, None),
            P(),
            P(),
            P(),
            P("tile"),
            P(None, None, "chan"),
            P(),
            P(None, "tile", "chan"),
        ),
        out_specs=(
            P(None, "tile", "chan"),
            P(None, "tile", None, "chan"),
            P(None, None, "chan"),
            P("chan", None),
        ),
        check_vma=False,
    )
```

```python
import math

import jax
import jax.numpy as jnp
from jax import lax
from jax.experimental import pallas as pl
from jax.experimental.pallas import tpu as pltpu
from jax.sharding import PartitionSpec as P

TILE_EDGE = 32


def turn_kernel(kernel, turn, direction):
    turned = jnp.zeros_like(kernel)
    for quarter in range(4):
        turned = turned + jnp.where(
            turn == quarter, jnp.rot90(kernel, direction * quarter, axes=(0, 1)), 0.0
        )
    return turned


def stencil_apply(field, kernel):
    shape_out = (field.shape[0], TILE_EDGE, TILE_EDGE, field.shape[3])
    hidden = jnp.zeros(shape_out, jnp.float32)
    for row_off in range(3):
        for col_off in range(3):
            window = field[
                :, row_off : row_off + TILE_EDGE, col_off : col_off + TILE_EDGE, :
            ].astype(jnp.float32)
            hidden = hidden + kernel[row_off, col_off] * window
    return hidden


def stencil_grads(field, kernel, grad_hidden):
    tap_rows = []
    grad_field = jnp.zeros(field.shape, jnp.float32)
    for row_off in range(3):
        tap_cols = []
        for col_off in range(3):
            window = field[
                :, row_off : row_off + TILE_EDGE, col_off : col_off + TILE_EDGE, :
            ].astype(jnp.float32)
            tap_cols.append(jnp.sum(window * grad_hidden, axis=(0, 1, 2)))
            spread = kernel[row_off, col_off] * grad_hidden
            grad_field = grad_field + jnp.pad(
                spread, ((0, 0), (row_off, 2 - row_off), (col_off, 2 - col_off), (0, 0))
            )
        tap_rows.append(jnp.stack(tap_cols))
    return (jnp.stack(tap_rows), grad_field)


CHUNKS = 4


def greet():
    barrier = pltpu.get_barrier_semaphore()
    met = 0
    for axis in ("tile", "chan"):
        total, here = lax.axis_size(axis), lax.axis_index(axis)
        for step in range(1, total):
            pl.semaphore_signal(
                barrier,
                inc=1,
                device_id={axis: lax.rem(here + step, total)},
                device_id_type=pl.DeviceIdType.MESH,
            )
            met += 1
    pl.semaphore_wait(barrier, met)


def send(src, dst, sems, place, where):
    copy = pltpu.make_async_remote_copy(
        src_ref=src,
        dst_ref=dst,
        send_sem=sems.at[(0, *place)],
        recv_sem=sems.at[(1, *place)],
        device_id=where,
        device_id_type=pl.DeviceIdType.MESH,
    )
    return copy


def swap_start(src, dst, rows, sems, spread):
    total, here = lax.axis_size("tile"), lax.axis_index("tile")
    into = pl.ds(pl.multiple_of(here * rows, rows), rows)
    own = src if spread else src.at[into]
    copies = [pltpu.make_async_copy(own, dst.at[into], sems.at[0, 0])]
    for step in range(1, total):
        peer = lax.rem(here + step, total)
        part = src if spread else src.at[pl.ds(pl.multiple_of(peer * rows, rows), rows)]
        copies.append(send(part, dst.at[into], sems, (step,), {"tile": peer}))
    for copy in copies:
        copy.start()
    return copies


def wait_all(copies):
    for copy in copies:
        copy.wait()


def line_gather(own, full, sems, local_sem, between):
    total, here = lax.axis_size("chan"), lax.axis_index("chan")
    wide, rows = own.shape[1], own.shape[0] // CHUNKS

    def at(ref, who, chunk):
        return ref.at[
            pl.ds(chunk * rows, rows), pl.ds(pl.multiple_of(who * wide, wide), wide)
        ]

    def hop(way, step, chunk):
        shift = 1 - 2 * way
        who = jnp.clip(here - shift * step, 0, total - 1)
        src = own.at[pl.ds(chunk * rows, rows)] if step == 0 else at(full, who, chunk)
        return send(
            src,
            at(full, who, chunk),
            sems,
            (way, step, chunk),
            {"chan": jnp.clip(here + shift, 0, total - 1)},
        )

    def far(way, step):
        return here >= step if way == 0 else here <= total - 1 - step

    def sends(way, step):
        return far(way, step) & (here < total - 1 if way == 0 else here > 0)

    local = pltpu.make_async_copy(
        own, full.at[:, pl.ds(pl.multiple_of(here * wide, wide), wide)], local_sem
    )
    local.start()
    for step in range(total):
        for chunk in range(CHUNKS):
            for way in range(2):
                if step > 0:

                    @pl.when(far(way, step))
                    def _(way=way, step=step, chunk=chunk):
                        hop(way, step - 1, chunk).wait_recv()

                if step < total - 1:

                    @pl.when(sends(way, step))
                    def _(way=way, step=step, chunk=chunk):
                        hop(way, step, chunk).start()

        if step in between:
            between[step]()
    for step in range(total - 1):
        for chunk in range(CHUNKS):
            for way in range(2):

                @pl.when(sends(way, step))
                def _(way=way, step=step, chunk=chunk):
                    hop(way, step, chunk).wait_send()

    local.wait()


def first_kernel(
    out_ref,
    own_ref,
    source_ref,
    weights_ref,
    column_ref,
    in_ref,
    full_ref,
    mapped_ref,
    pick_ref,
    weights,
    slots,
    picked,
    swap_sems,
    line_sems,
    local_sem,
    weights_sem,
):
    fetch = pltpu.make_async_copy(weights_ref, weights, weights_sem)
    fetch.start()
    greet()
    rows = out_ref.shape[0] // lax.axis_size("tile")
    copies = swap_start(out_ref, in_ref, rows, swap_sems, False)
    terms, filled = pick_ref.shape
    seg = out_ref.shape[0] // filled

    def remap():
        shape = (terms, terms)
        source = column_ref[...]
        earlier = lax.broadcasted_iota(jnp.int32, shape, 1) <= lax.broadcasted_iota(
            jnp.int32, shape, 0
        )
        same = (source == source_ref[...]) & earlier
        rank = jnp.sum(jnp.where(same, 1.0, 0.0), axis=1, keepdims=True) - 1.0
        capacity = filled // lax.axis_size("tile")
        slot = source.astype(jnp.float32) * capacity + rank
        slot = jnp.where(source >= 0, slot, -1.0)
        ids = lax.broadcasted_iota(jnp.int32, (terms, filled), 1).astype(jnp.float32)
        pick_ref[...] = jnp.where(slot == ids, 1.0, 0.0).astype(jnp.bfloat16)
        wait_all(copies)
        slots[...] = in_ref[...].astype(jnp.float32)
        for point in range(seg):
            part = slots[pl.ds(point, filled, stride=seg), :].astype(jnp.bfloat16)
            picked[pl.ds(point, terms, stride=seg), :] = jnp.dot(
                pick_ref[...], part, preferred_element_type=jnp.float32
            )
        fetch.wait()
        mapped_ref[...] = jnp.dot(
            weights[...],
            picked[...].astype(jnp.bfloat16),
            preferred_element_type=jnp.float32,
        ).astype(jnp.bfloat16)

    last = lax.axis_size("chan") - 2
    line_gather(own_ref, full_ref, line_sems, local_sem, {last: remap})


def second_kernel(
    grad_ref,
    own_ref,
    pick_ref,
    weights_ref,
    mix_ref,
    taps_ref,
    in_ref,
    full_ref,
    mix_out,
    taps_out,
    mix_parts,
    mix_own,
    taps_parts,
    weights,
    terms_ref,
    slots,
    out_ref,
    swap_sems,
    line_sems,
    mix_sems,
    back_sems,
    taps_sems,
    local_sem,
    weights_sem,
):
    fetch = pltpu.make_async_copy(weights_ref, weights, weights_sem)
    fetch.start()
    greet()
    total = lax.axis_size("tile")
    mix_rows = mix_ref.shape[0] // total
    mix_copies = swap_start(mix_ref, mix_parts, mix_rows, mix_sems, False)
    taps_copies = swap_start(taps_ref, taps_parts, taps_ref.shape[0], taps_sems, True)
    copies, back = [], []
    terms, filled = pick_ref.shape
    seg = out_ref.shape[0] // filled

    def unmap():
        fetch.wait()
        turned = lax.dot_general(
            grad_ref[...],
            weights[...],
            (((0,), (0,)), ((), ())),
            preferred_element_type=jnp.float32,
        )
        terms_ref[...] = turned.T
        for point in range(seg):
            part = terms_ref[pl.ds(point, terms, stride=seg), :].astype(jnp.bfloat16)
            slots[pl.ds(point, filled, stride=seg), :] = lax.dot_general(
                pick_ref[...],
                part,
                (((0,), (0,)), ((), ())),
                preferred_element_type=jnp.float32,
            )
        out_ref[...] = slots[...].astype(jnp.bfloat16)
        rows = out_ref.shape[0] // total
        copies.extend(swap_start(out_ref, in_ref, rows, swap_sems, False))

    def reduce():
        wait_all(mix_copies)
        summed = mix_parts[0:mix_rows]
        for part in range(1, total):
            summed = summed + mix_parts[part * mix_rows : (part + 1) * mix_rows]
        mix_own[...] = summed.astype(mix_own.dtype)
        back.extend(swap_start(mix_own, mix_out, mix_rows, back_sems, True))

    line_gather(own_ref, full_ref, line_sems, local_sem, {0: unmap, 1: reduce})
    wait_all(taps_copies)
    tap_rows = taps_ref.shape[0]
    taps = taps_parts[0:tap_rows]
    for part in range(1, total):
        taps = taps + taps_parts[part * tap_rows : (part + 1) * tap_rows]
    taps_out[...] = taps
    wait_all(back)
    wait_all(copies)


def call(kernel, shapes, scratch, sems, collective_id, *operands):
    vmem = pl.BlockSpec(memory_space=pltpu.VMEM)
    line = (2, 2, lax.axis_size("chan"), CHUNKS)
    return pl.pallas_call(
        kernel,
        out_shape=[jax.ShapeDtypeStruct(*one) for one in shapes],
        in_specs=[
            pl.BlockSpec(memory_space=pltpu.HBM) if at == 3 else vmem
            for at in range(len(operands))
        ],
        out_specs=[vmem] * len(shapes),
        scratch_shapes=[
            *[pltpu.VMEM(*one) for one in scratch],
            pltpu.SemaphoreType.DMA((2, lax.axis_size("tile"))),
            pltpu.SemaphoreType.DMA(line),
            *[pltpu.SemaphoreType.DMA((2, lax.axis_size("tile")))] * sems,
            pltpu.SemaphoreType.DMA,
            pltpu.SemaphoreType.DMA,
        ],
        compiler_params=pltpu.CompilerParams(
            collective_id=collective_id,
            has_side_effects=True,
            vmem_limit_bytes=52 * 2**20,
        ),
    )(*operands)


def body(
    latlon,
    remap_weights,
    term_source,
    term_block,
    term_count,
    rotation,
    depthwise,
    pointwise,
    cotangent,
):
    tile_now = lax.axis_index("tile")
    tile_total = lax.axis_size("tile")
    chan_now = lax.axis_index("chan")
    batch_rows, block_total, seg_len, chan_local = latlon.shape
    terms_max = term_source.shape[1]
    capacity = 3 * terms_max // (2 * tile_total)
    ext_edge = TILE_EDGE + 2
    tile_cells = TILE_EDGE * TILE_EDGE
    flat_rows = batch_rows * tile_cells
    positions = jnp.arange(terms_max, dtype=jnp.int32)
    in_use = positions[None, :] < term_count[:, None]
    mine = in_use & (term_source == tile_now)
    before = (positions[:, None] <= positions[None, :]).astype(jnp.bfloat16)
    send_rank = jnp.dot(mine.astype(jnp.bfloat16), before, preferred_element_type=jnp.float32)
    send_rank = send_rank.astype(jnp.int32) - 1
    slot_ids = jnp.arange(capacity, dtype=jnp.int32)
    slot_hits = mine[:, None, :] & (send_rank[:, None, :] == slot_ids[None, :, None])
    slot_block = (jnp.sum(jnp.where(slot_hits, term_block[:, None, :] + 1, 0), axis=2) - 1).reshape(-1)
    blocks = jnp.arange(block_total, dtype=jnp.int32)
    send_pick = (slot_block[:, None] == blocks[None, :]).astype(jnp.bfloat16)
    outgoing = jnp.einsum("nb,abkc->ankc", send_pick, latlon, preferred_element_type=jnp.float32)
    outgoing = outgoing.astype(jnp.bfloat16)
    tile_mask = (jnp.arange(tile_total) == tile_now)[:, None]
    own_source = jnp.sum(jnp.where(tile_mask, term_source, 0), axis=0)
    own_count = jnp.sum(jnp.where(tile_mask[:, 0], term_count, 0))
    own_use = positions < own_count
    named = jnp.where(own_use, own_source, -1)
    weights = remap_weights[0]
    ext_cells = weights.shape[0]
    term_pts = weights.shape[1]
    slot_shape = outgoing.shape
    upstream = cotangent.reshape(flat_rows, chan_local)
    chan_total = lax.axis_size("chan")
    outgoing = outgoing.reshape(-1, chan_local)
    whole_shape = (flat_rows, chan_total * chan_local)
    points = (term_pts, chan_local)
    _, piece, remapped, recv_pick = call(
        first_kernel,
        (
            (outgoing.shape, jnp.bfloat16),
            (whole_shape, jnp.bfloat16),
            ((ext_cells, chan_local), jnp.bfloat16),
            ((terms_max, tile_total * capacity), jnp.bfloat16),
        ),
        (
            (weights.shape, jnp.bfloat16),
            (outgoing.shape, jnp.float32),
            (points, jnp.float32),
        ),
        0,
        0,
        outgoing,
        upstream,
        named[None, :],
        weights,
        named[:, None],
    )
    field = remapped.reshape(batch_rows, ext_edge, ext_edge, chan_local)
    turn = rotation[0]
    kernel = turn_kernel(depthwise.astype(jnp.float32), turn, 1)
    hidden = stencil_apply(field, kernel)
    active = jax.nn.silu(hidden).astype(jnp.bfloat16).reshape(flat_rows, chan_local)
    own_rows = lax.dynamic_slice_in_dim(pointwise, chan_now * chan_local, chan_local, 0)
    own_cols = lax.dynamic_slice_in_dim(pointwise, chan_now * chan_local, chan_local, 1)
    grad_active = lax.dot_general(
        piece, own_rows, (((1,), (1,)), ((), ())), preferred_element_type=jnp.float32
    )
    block_grad = lax.dot_general(
        active, piece, (((0,), (0,)), ((), ())), preferred_element_type=jnp.float32
    )
    grad_mix = block_grad
    grad_active, grad_mix = (grad_active, grad_mix)
    sigma = jax.nn.sigmoid(hidden)
    grad_hidden = grad_active.reshape(hidden.shape) * sigma * (1.0 + hidden * (1.0 - sigma))
    grad_turned, grad_field = stencil_grads(field, kernel, grad_hidden)
    grad_field = grad_field.astype(jnp.bfloat16).reshape(ext_cells, chan_local)
    grad_kernel = turn_kernel(grad_turned, turn, -1).reshape(9, chan_local)
    grad_kernel = jnp.pad(grad_kernel, ((0, 7), (0, 0)))
    grad_mix = jnp.concatenate(
        [grad_mix[:, i * chan_local : (i + 1) * chan_local] for i in range(chan_total)]
    )
    mix_rows = grad_mix.shape[0] // tile_total
    mix_type = jnp.bfloat16 if mix_rows % 16 == 0 else jnp.float32
    arrived, active_all, mix_sum, kernel_sum = call(
        second_kernel,
        (
            (outgoing.shape, jnp.bfloat16),
            (whole_shape, jnp.bfloat16),
            (grad_mix.shape, mix_type),
            (grad_kernel.shape, jnp.float32),
        ),
        (
            (grad_mix.shape, jnp.float32),
            ((mix_rows, chan_local), mix_type),
            ((tile_total * grad_kernel.shape[0], chan_local), jnp.float32),
            (weights.shape, jnp.bfloat16),
            (points, jnp.float32),
            (outgoing.shape, jnp.float32),
            (outgoing.shape, jnp.bfloat16),
        ),
        3,
        1,
        grad_field,
        active,
        recv_pick,
        weights,
        grad_mix,
        grad_kernel,
    )
    mixed = jnp.dot(active_all, own_cols, preferred_element_type=jnp.float32)
    coupled = mixed.astype(jnp.bfloat16).reshape(batch_rows, tile_cells, chan_local)
    arrived = arrived.reshape(slot_shape)
    mix_sum = mix_sum.astype(jnp.float32)
    mix_sum = jnp.concatenate(
        [mix_sum[i * chan_local : (i + 1) * chan_local] for i in range(chan_total)], axis=1
    )
    kernel_sum = kernel_sum[:9].reshape(3, 3, chan_local)
    summed = jnp.einsum("nb,ankc->abkc", send_pick, arrived, preferred_element_type=jnp.float32)
    grad_latlon = summed.astype(jnp.bfloat16)
    factor = 1.0 / math.sqrt(batch_rows * tile_cells * tile_total)
    return (coupled, grad_latlon, kernel_sum * factor, mix_sum * factor)


def solution(mesh):
    return jax.shard_map(
        body,
        mesh=mesh,
        in_specs=(
            P(None, "tile", None, "chan"),
            P("tile", None, None),
            P(),
            P(),
            P(),
            P("tile"),
            P(None, None, "chan"),
            P(),
            P(None, "tile", "chan"),
        ),
        out_specs=(
            P(None, "tile", "chan"),
            P(None, "tile", None, "chan"),
            P(None, None, "chan"),
            P("chan", None),
        ),
        check_vma=False,
    )
```

```python
import math

import jax
import jax.numpy as jnp
from jax import lax
from jax.experimental import pallas as pl
from jax.experimental.pallas import tpu as pltpu
from jax.sharding import PartitionSpec as P

TILE_EDGE = 32


def turn_kernel(kernel, turn, direction):
    turned = jnp.zeros_like(kernel)
    for quarter in range(4):
        turned = turned + jnp.where(
            turn == quarter, jnp.rot90(kernel, direction * quarter, axes=(0, 1)), 0.0
        )
    return turned


def stencil_apply(field, kernel):
    shape_out = (field.shape[0], TILE_EDGE, TILE_EDGE, field.shape[3])
    hidden = jnp.zeros(shape_out, jnp.float32)
    for row_off in range(3):
        for col_off in range(3):
            window = field[
                :, row_off : row_off + TILE_EDGE, col_off : col_off + TILE_EDGE, :
            ].astype(jnp.float32)
            hidden = hidden + kernel[row_off, col_off] * window
    return hidden


def stencil_grads(field, kernel, grad_hidden):
    tap_rows = []
    grad_field = jnp.zeros(field.shape, jnp.float32)
    for row_off in range(3):
        tap_cols = []
        for col_off in range(3):
            window = field[
                :, row_off : row_off + TILE_EDGE, col_off : col_off + TILE_EDGE, :
            ].astype(jnp.float32)
            tap_cols.append(jnp.sum(window * grad_hidden, axis=(0, 1, 2)))
            spread = kernel[row_off, col_off] * grad_hidden
            grad_field = grad_field + jnp.pad(
                spread, ((0, 0), (row_off, 2 - row_off), (col_off, 2 - col_off), (0, 0))
            )
        tap_rows.append(jnp.stack(tap_cols))
    return (jnp.stack(tap_rows), grad_field)


CHUNKS = 4


def greet():
    barrier = pltpu.get_barrier_semaphore()
    met = 0
    for axis in ("tile", "chan"):
        total, here = lax.axis_size(axis), lax.axis_index(axis)
        for step in range(1, total):
            pl.semaphore_signal(
                barrier,
                inc=1,
                device_id={axis: lax.rem(here + step, total)},
                device_id_type=pl.DeviceIdType.MESH,
            )
            met += 1
    pl.semaphore_wait(barrier, met)


def send(src, dst, sems, place, where):
    copy = pltpu.make_async_remote_copy(
        src_ref=src,
        dst_ref=dst,
        send_sem=sems.at[(0, *place)],
        recv_sem=sems.at[(1, *place)],
        device_id=where,
        device_id_type=pl.DeviceIdType.MESH,
    )
    return copy


def swap_start(src, dst, rows, sems, spread):
    total, here = lax.axis_size("tile"), lax.axis_index("tile")
    into = pl.ds(pl.multiple_of(here * rows, rows), rows)
    own = src if spread else src.at[into]
    copies = [pltpu.make_async_copy(own, dst.at[into], sems.at[0, 0])]
    for step in range(1, total):
        peer = lax.rem(here + step, total)
        part = src if spread else src.at[pl.ds(pl.multiple_of(peer * rows, rows), rows)]
        copies.append(send(part, dst.at[into], sems, (step,), {"tile": peer}))
    for copy in copies:
        copy.start()
    return copies


def wait_all(copies):
    for copy in copies:
        copy.wait()


def line_gather(own, full, sems, local_sem, between):
    total, here = lax.axis_size("chan"), lax.axis_index("chan")
    wide, rows = own.shape[1], own.shape[0] // CHUNKS

    def at(ref, who, chunk):
        return ref.at[
            pl.ds(chunk * rows, rows), pl.ds(pl.multiple_of(who * wide, wide), wide)
        ]

    def hop(way, step, chunk):
        shift = 1 - 2 * way
        who = jnp.clip(here - shift * step, 0, total - 1)
        src = own.at[pl.ds(chunk * rows, rows)] if step == 0 else at(full, who, chunk)
        return send(
            src,
            at(full, who, chunk),
            sems,
            (way, step, chunk),
            {"chan": jnp.clip(here + shift, 0, total - 1)},
        )

    def far(way, step):
        return here >= step if way == 0 else here <= total - 1 - step

    def sends(way, step):
        return far(way, step) & (here < total - 1 if way == 0 else here > 0)

    local = pltpu.make_async_copy(
        own, full.at[:, pl.ds(pl.multiple_of(here * wide, wide), wide)], local_sem
    )
    local.start()
    for step in range(total):
        for chunk in range(CHUNKS):
            for way in range(2):
                if step > 0:

                    @pl.when(far(way, step))
                    def _(way=way, step=step, chunk=chunk):
                        hop(way, step - 1, chunk).wait_recv()

                if step < total - 1:

                    @pl.when(sends(way, step))
                    def _(way=way, step=step, chunk=chunk):
                        hop(way, step, chunk).start()

        if step in between:
            between[step]()
    for step in range(total - 1):
        for chunk in range(CHUNKS):
            for way in range(2):

                @pl.when(sends(way, step))
                def _(way=way, step=step, chunk=chunk):
                    hop(way, step, chunk).wait_send()

    local.wait()


def first_kernel(
    out_ref,
    own_ref,
    source_ref,
    weights_ref,
    in_ref,
    full_ref,
    mapped_ref,
    pick_ref,
    weights,
    slots,
    picked,
    swap_sems,
    line_sems,
    local_sem,
    weights_sem,
):
    fetch = pltpu.make_async_copy(weights_ref, weights, weights_sem)
    fetch.start()
    greet()
    rows = out_ref.shape[0] // lax.axis_size("tile")
    copies = swap_start(out_ref, in_ref, rows, swap_sems, False)
    terms, filled = pick_ref.shape
    seg = out_ref.shape[0] // filled

    def remap():
        shape = (terms, terms)
        here = lax.axis_index("tile")
        tiles = lax.broadcasted_iota(jnp.int32, source_ref.shape, 0)
        named = jnp.where(tiles == here, source_ref[...].astype(jnp.float32), 0.0)
        row = jnp.sum(named, axis=0, keepdims=True)
        across = lax.broadcasted_iota(jnp.int32, shape, 1)
        down = lax.broadcasted_iota(jnp.int32, shape, 0)
        source = jnp.sum(jnp.where(across == down, row, 0.0), axis=1, keepdims=True)
        same = (source == row) & (across <= down)
        rank = jnp.sum(jnp.where(same, 1.0, 0.0), axis=1, keepdims=True) - 1.0
        capacity = filled // lax.axis_size("tile")
        slot = source * capacity + rank
        slot = jnp.where(source >= 0.0, slot, -1.0)
        ids = lax.broadcasted_iota(jnp.int32, (terms, filled), 1).astype(jnp.float32)
        pick_ref[...] = jnp.where(slot == ids, 1.0, 0.0).astype(jnp.bfloat16)
        wait_all(copies)
        slots[...] = in_ref[...].astype(jnp.float32)
        for point in range(seg):
            part = slots[pl.ds(point, filled, stride=seg), :].astype(jnp.bfloat16)
            picked[pl.ds(point, terms, stride=seg), :] = jnp.dot(
                pick_ref[...], part, preferred_element_type=jnp.float32
            )
        fetch.wait()
        mapped_ref[...] = jnp.dot(
            weights[...],
            picked[...].astype(jnp.bfloat16),
            preferred_element_type=jnp.float32,
        ).astype(jnp.bfloat16)

    last = lax.axis_size("chan") - 2
    line_gather(own_ref, full_ref, line_sems, local_sem, {last: remap})


def second_kernel(
    grad_ref,
    own_ref,
    pick_ref,
    weights_ref,
    mix_ref,
    taps_ref,
    in_ref,
    full_ref,
    mix_out,
    taps_out,
    mix_parts,
    mix_own,
    taps_parts,
    weights,
    terms_ref,
    slots,
    out_ref,
    swap_sems,
    line_sems,
    mix_sems,
    back_sems,
    taps_sems,
    local_sem,
    weights_sem,
):
    fetch = pltpu.make_async_copy(weights_ref, weights, weights_sem)
    fetch.start()
    greet()
    total = lax.axis_size("tile")
    mix_rows = mix_ref.shape[0] // total
    mix_copies = swap_start(mix_ref, mix_parts, mix_rows, mix_sems, False)
    taps_copies = swap_start(taps_ref, taps_parts, taps_ref.shape[0], taps_sems, True)
    copies, back = [], []
    terms, filled = pick_ref.shape
    seg = out_ref.shape[0] // filled

    def unmap():
        fetch.wait()
        turned = lax.dot_general(
            grad_ref[...],
            weights[...],
            (((0,), (0,)), ((), ())),
            preferred_element_type=jnp.float32,
        )
        terms_ref[...] = turned.T
        for point in range(seg):
            part = terms_ref[pl.ds(point, terms, stride=seg), :].astype(jnp.bfloat16)
            slots[pl.ds(point, filled, stride=seg), :] = lax.dot_general(
                pick_ref[...],
                part,
                (((0,), (0,)), ((), ())),
                preferred_element_type=jnp.float32,
            )
        out_ref[...] = slots[...].astype(jnp.bfloat16)
        rows = out_ref.shape[0] // total
        copies.extend(swap_start(out_ref, in_ref, rows, swap_sems, False))

    def reduce():
        wait_all(mix_copies)
        summed = mix_parts[0:mix_rows]
        for part in range(1, total):
            summed = summed + mix_parts[part * mix_rows : (part + 1) * mix_rows]
        mix_own[...] = summed.astype(mix_own.dtype)
        back.extend(swap_start(mix_own, mix_out, mix_rows, back_sems, True))

    line_gather(own_ref, full_ref, line_sems, local_sem, {0: unmap, 1: reduce})
    wait_all(taps_copies)
    tap_rows = taps_ref.shape[0]
    taps = taps_parts[0:tap_rows]
    for part in range(1, total):
        taps = taps + taps_parts[part * tap_rows : (part + 1) * tap_rows]
    taps_out[...] = taps
    wait_all(back)
    wait_all(copies)


def call(kernel, shapes, scratch, sems, collective_id, *operands):
    vmem = pl.BlockSpec(memory_space=pltpu.VMEM)
    line = (2, 2, lax.axis_size("chan"), CHUNKS)
    return pl.pallas_call(
        kernel,
        out_shape=[jax.ShapeDtypeStruct(*one) for one in shapes],
        in_specs=[
            pl.BlockSpec(memory_space=pltpu.HBM) if at == 3 else vmem
            for at in range(len(operands))
        ],
        out_specs=[vmem] * len(shapes),
        scratch_shapes=[
            *[pltpu.VMEM(*one) for one in scratch],
            pltpu.SemaphoreType.DMA((2, lax.axis_size("tile"))),
            pltpu.SemaphoreType.DMA(line),
            *[pltpu.SemaphoreType.DMA((2, lax.axis_size("tile")))] * sems,
            pltpu.SemaphoreType.DMA,
            pltpu.SemaphoreType.DMA,
        ],
        compiler_params=pltpu.CompilerParams(
            collective_id=collective_id,
            has_side_effects=True,
            vmem_limit_bytes=49 * 2**20,
        ),
    )(*operands)


def body(
    latlon,
    remap_weights,
    term_source,
    term_block,
    term_count,
    rotation,
    depthwise,
    pointwise,
    cotangent,
):
    tile_now = lax.axis_index("tile")
    tile_total = lax.axis_size("tile")
    chan_now = lax.axis_index("chan")
    batch_rows, block_total, seg_len, chan_local = latlon.shape
    terms_max = term_source.shape[1]
    capacity = 3 * terms_max // (2 * tile_total)
    ext_edge = TILE_EDGE + 2
    tile_cells = TILE_EDGE * TILE_EDGE
    flat_rows = batch_rows * tile_cells
    positions = jnp.arange(terms_max, dtype=jnp.int32)
    in_use = positions[None, :] < term_count[:, None]
    mine = in_use & (term_source == tile_now)
    before = (positions[:, None] <= positions[None, :]).astype(jnp.bfloat16)
    send_rank = jnp.dot(mine.astype(jnp.bfloat16), before, preferred_element_type=jnp.float32)
    send_rank = send_rank.astype(jnp.int32) - 1
    slot_ids = jnp.arange(capacity, dtype=jnp.int32)
    slot_hits = mine[:, None, :] & (send_rank[:, None, :] == slot_ids[None, :, None])
    slot_block = (jnp.sum(jnp.where(slot_hits, term_block[:, None, :] + 1, 0), axis=2) - 1).reshape(-1)
    blocks = jnp.arange(block_total, dtype=jnp.int32)
    send_pick = (slot_block[:, None] == blocks[None, :]).astype(jnp.bfloat16)
    outgoing = jnp.einsum("nb,abkc->ankc", send_pick, latlon, preferred_element_type=jnp.float32)
    outgoing = outgoing.astype(jnp.bfloat16)
    named = jnp.where(in_use, term_source, -1)
    weights = remap_weights[0]
    ext_cells = weights.shape[0]
    term_pts = weights.shape[1]
    slot_shape = outgoing.shape
    upstream = cotangent.reshape(flat_rows, chan_local)
    chan_total = lax.axis_size("chan")
    outgoing = outgoing.reshape(-1, chan_local)
    whole_shape = (flat_rows, chan_total * chan_local)
    points = (term_pts, chan_local)
    _, piece, remapped, recv_pick = call(
        first_kernel,
        (
            (outgoing.shape, jnp.bfloat16),
            (whole_shape, jnp.bfloat16),
            ((ext_cells, chan_local), jnp.bfloat16),
            ((terms_max, tile_total * capacity), jnp.bfloat16),
        ),
        (
            (weights.shape, jnp.bfloat16),
            (outgoing.shape, jnp.float32),
            (points, jnp.float32),
        ),
        0,
        0,
        outgoing,
        upstream,
        named,
        weights,
    )
    field = remapped.reshape(batch_rows, ext_edge, ext_edge, chan_local)
    turn = rotation[0]
    kernel = turn_kernel(depthwise.astype(jnp.float32), turn, 1)
    hidden = stencil_apply(field, kernel)
    active = jax.nn.silu(hidden).astype(jnp.bfloat16).reshape(flat_rows, chan_local)
    own_rows = lax.dynamic_slice_in_dim(pointwise, chan_now * chan_local, chan_local, 0)
    own_cols = lax.dynamic_slice_in_dim(pointwise, chan_now * chan_local, chan_local, 1)
    grad_active = lax.dot_general(
        piece, own_rows, (((1,), (1,)), ((), ())), preferred_element_type=jnp.float32
    )
    block_grad = lax.dot_general(
        active, piece, (((0,), (0,)), ((), ())), preferred_element_type=jnp.float32
    )
    grad_mix = block_grad
    grad_active, grad_mix = (grad_active, grad_mix)
    sigma = jax.nn.sigmoid(hidden)
    grad_hidden = grad_active.reshape(hidden.shape) * sigma * (1.0 + hidden * (1.0 - sigma))
    grad_turned, grad_field = stencil_grads(field, kernel, grad_hidden)
    grad_field = grad_field.astype(jnp.bfloat16).reshape(ext_cells, chan_local)
    grad_kernel = turn_kernel(grad_turned, turn, -1).reshape(9, chan_local)
    grad_kernel = jnp.pad(grad_kernel, ((0, 7), (0, 0)))
    grad_mix = jnp.concatenate(
        [grad_mix[:, i * chan_local : (i + 1) * chan_local] for i in range(chan_total)]
    )
    mix_rows = grad_mix.shape[0] // tile_total
    mix_type = jnp.bfloat16 if mix_rows % 16 == 0 else jnp.float32
    arrived, active_all, mix_sum, kernel_sum = call(
        second_kernel,
        (
            (outgoing.shape, jnp.bfloat16),
            (whole_shape, jnp.bfloat16),
            (grad_mix.shape, mix_type),
            (grad_kernel.shape, jnp.float32),
        ),
        (
            (grad_mix.shape, jnp.float32),
            ((mix_rows, chan_local), mix_type),
            ((tile_total * grad_kernel.shape[0], chan_local), jnp.float32),
            (weights.shape, jnp.bfloat16),
            (points, jnp.float32),
            (outgoing.shape, jnp.float32),
            (outgoing.shape, jnp.bfloat16),
        ),
        3,
        1,
        grad_field,
        active,
        recv_pick,
        weights,
        grad_mix,
        grad_kernel,
    )
    mixed = jnp.dot(active_all, own_cols, preferred_element_type=jnp.float32)
    coupled = mixed.astype(jnp.bfloat16).reshape(batch_rows, tile_cells, chan_local)
    arrived = arrived.reshape(slot_shape)
    mix_sum = mix_sum.astype(jnp.float32)
    mix_sum = jnp.concatenate(
        [mix_sum[i * chan_local : (i + 1) * chan_local] for i in range(chan_total)], axis=1
    )
    kernel_sum = kernel_sum[:9].reshape(3, 3, chan_local)
    summed = jnp.einsum("nb,ankc->abkc", send_pick, arrived, preferred_element_type=jnp.float32)
    grad_latlon = summed.astype(jnp.bfloat16)
    factor = 1.0 / math.sqrt(batch_rows * tile_cells * tile_total)
    return (coupled, grad_latlon, kernel_sum * factor, mix_sum * factor)


def solution(mesh):
    return jax.shard_map(
        body,
        mesh=mesh,
        in_specs=(
            P(None, "tile", None, "chan"),
            P("tile", None, None),
            P(),
            P(),
            P(),
            P("tile"),
            P(None, None, "chan"),
            P(),
            P(None, "tile", "chan"),
        ),
        out_specs=(
            P(None, "tile", "chan"),
            P(None, "tile", None, "chan"),
            P(None, None, "chan"),
            P("chan", None),
        ),
        check_vma=False,
    )
```
